32 devices in a mesh: occ: 4 (over y, core), virt: 4 (over z), rep: 2 (over x).
Axes of the slice: x: 2, y: 2, z: 4, core: 2. Of those that a mesh axis runs over, the one named last changes fastest.
Arguments:
- amplitudes: bfloat16 [4096, 1920], P(('occ', 'rep'), 'virt'), may hold values from -6 to 6
- integrals: bfloat16 [1920, 1024], P(('occ', 'rep'), 'virt'), may hold values from -0.375 to 0.375
- cd_irrep: int32 [1920], P(('occ', 'rep')), may hold values from 0 to 7
- ab_irrep: int32 [1024], P('virt'), may hold values from 0 to 7
Outputs:
- residual: float32 [4096, 1024], P(('occ', 'rep'), 'virt')
The draws below stay inside these ranges and needn't reach their ends.
Inputs may be any that keep to these rules, and one draw needn't show every extreme that they name: `cd_irrep`: irreps of the eight D2h irreducible representations. `ab_irrep`: irreps of the eight D2h irreducible representations.
All inputs are finite; a program needn't handle non-finite values.
Results may differ from the reference program's by a relative error of at most 0.0003.
Values may be sent and summed in bfloat16 or wider, within the bound.
A program may use at most 64 MiB of HBM per device.

```python
import jax
import jax.numpy as jnp

OPAIR = 4096
CD = 1920
AB = 1024


def touch_ends(drawn, own_key, least, high):
    longest = drawn.shape.index(max(drawn.shape))
    spots = []
    for shift in (0, 1):
        where = [jax.random.randint(jax.random.fold_in(own_key, axis), (), 0, length) for axis, length in enumerate(drawn.shape)]
        where[longest] = (where[longest] + shift) % drawn.shape[longest]
        spots.append(tuple(where))
    return drawn.at[spots[0]].set(least).at[spots[1]].set(high)


def shard_levels(rng, shape, pieces, smallest, largest):
    level = 1.0
    for dim, blocks in pieces:
        draws = jax.random.uniform(jax.random.fold_in(jax.random.fold_in(rng, 6), dim), (blocks,), jnp.float32, smallest / len(pieces), largest / len(pieces))
        level = level * jnp.repeat(jnp.exp(draws), shape[dim] // blocks).reshape((-1,) + (1,) * (len(shape) - 1 - dim))
    return level


def noise(own_key, extent, deviation, most, pieces=(), kind=jnp.bfloat16):
    drawn = jax.random.normal(own_key, extent, jnp.float32) * deviation
    if len(pieces) > 0:
        drawn = shard_levels(own_key, extent, pieces, -0.22, 0.18) * drawn
    return jnp.clip(drawn, min=-most, max=most).astype(kind)


def setup_inputs(seed: int = 0) -> dict:
    key_list = jax.random.split(jax.random.key(seed), 5)
    return {
        "amplitudes": noise(key_list[0], (OPAIR, CD), 1.0, 6.0, ((0, 8), (1, 4))),
        "integrals": noise(key_list[1], (CD, AB), (CD // 8) ** -0.5, 0.375, ((0, 8), (1, 4))),
        "cd_irrep": touch_ends(jax.random.randint(key_list[2], (CD,), 0, 8), jax.random.fold_in(key_list[2], 1), 0, 7).astype(jnp.int32),
        "ab_irrep": touch_ends(jax.random.randint(key_list[3], (AB,), 0, 8), jax.random.fold_in(key_list[3], 1), 0, 7).astype(jnp.int32),
    }


def reference(amplitudes, integrals, cd_irrep, ab_irrep):
    allowed = cd_irrep[:, None] == ab_irrep[None, :]
    masked = jnp.where(allowed, integrals, jnp.zeros_like(integrals))
    return jnp.dot(amplitudes, masked, preferred_element_type=jnp.float32)
```

```python
import jax
import jax.numpy as jnp
from jax import lax
from jax.sharding import PartitionSpec as P


def local(amplitudes, integrals, cd_irrep, ab_irrep):
    allowed = cd_irrep[:, None] == ab_irrep[None, :]
    masked = jnp.where(allowed, integrals, jnp.zeros_like(integrals))
    rows = lax.all_gather(masked, ("occ", "rep"), axis=0, tiled=True)
    columns = lax.all_gather(amplitudes, "virt", axis=1, tiled=True)
    return jnp.dot(columns, rows, preferred_element_type=jnp.float32)


def solution(mesh):
    in_specs = (P(("occ", "rep"), "virt"), P(("occ", "rep"), "virt"), P(("occ", "rep")), P("virt"))
    out_specs = P(("occ", "rep"), "virt")
    return jax.shard_map(local, mesh=mesh, in_specs=in_specs, out_specs=out_specs, check_vma=False)
```

```python
import functools

import jax
import jax.numpy as jnp
from jax import lax
from jax.experimental import pallas as pl
from jax.experimental.pallas import tpu as pltpu
from jax.sharding import PartitionSpec as P

MESH = pl.DeviceIdType.MESH
NV = 4
NO = 4
NR = 2
CHUNKS = 4
ORDER = ((3, 2, 1, 0), (3, 0, 2, 1), (0, 3, 1, 2), (0, 1, 2, 3))
PEERS = [(do, dr) for do in range(NO) for dr in range(NR) if (do, dr) != (0, 0)]


def schedule(zz):
    steps = []
    if zz in (0, NV - 1):
        for v in ORDER[zz][:-1]:
            steps += [(v, c) for c in range(CHUNKS)]
    else:
        a, b, near, _ = ORDER[zz]
        timed = []
        for c in range(CHUNKS):
            timed += [(c, 0, a, c), (c + 1.5, 1, b, c), (c + CHUNKS + 0.7, 2, near, c)]
        steps = [(v, c) for _, _, v, c in sorted(timed)]
    return steps + [(zz, c) for c in range(CHUNKS)]


def kernel(t_ref, i_ref, cd_ref, ab_ref, out_ref, masked, ints, full, psend, ssend, precv, srecv,
           mine_send, mine_recv, relay_send, relay_recv, p_ssem, s_ssem, p_rsem, s_rsem):
    o, z, r = lax.axis_index("occ"), lax.axis_index("virt"), lax.axis_index("rep")
    core = o % 2
    half = o // 2
    rows, depth = t_ref.shape
    chunk = rows // CHUNKS
    part = depth // NR

    barrier = pltpu.get_barrier_semaphore()
    friends = 0
    for do, dr in PEERS:
        pl.semaphore_signal(barrier, inc=1, device_id=((o + do) % NO, z, (r + dr) % NR), device_id_type=MESH)
        friends += 1
    for dz in range(1, NV):
        for do in (0, 2):
            pl.semaphore_signal(barrier, inc=1, device_id=((o + do) % NO, (z + dz) % NV, r), device_id_type=MESH)
            friends += 1

    cd = cd_ref[...]
    ab = ab_ref[...]
    one_cd = (lax.broadcasted_iota(jnp.int32, (8, cd.shape[1]), 0) == cd).astype(jnp.float32)
    one_ab = (lax.broadcasted_iota(jnp.int32, (8, ab.shape[1]), 0) == ab).astype(jnp.float32)
    same = lax.dot_general(one_cd, one_ab, (((0,), (0,)), ((), ())), preferred_element_type=jnp.float32)
    kept = jnp.where(same > 0.5, i_ref[...].astype(jnp.float32), 0.0).astype(jnp.bfloat16)
    width = kept.shape[1] // 2
    masked[0] = kept[:, :width]
    masked[1] = kept[:, width:]

    pl.semaphore_wait(barrier, friends)

    def first(h):
        return pltpu.make_async_remote_copy(
            src_ref=masked.at[h], dst_ref=ints.at[z, r, h], send_sem=mine_send.at[h], recv_sem=mine_recv.at[z],
            device_id=(2 * h + core, o, r), device_id_type=MESH)

    stays = [(z == o) & (half == h) for h in range(2)]
    for h in range(2):
        @pl.when(jnp.logical_not(stays[h]))
        def _():
            first(h).start()

        @pl.when(stays[h])
        def _():
            ints[z, r, h] = masked[h]

    relays = core == z % 2

    def hand(v, k):
        do, dr = PEERS[k]
        return pltpu.make_async_remote_copy(
            src_ref=ints.at[v, r, half], dst_ref=ints.at[v, r, half], send_sem=relay_send.at[v, k],
            recv_sem=relay_recv.at[v, r, half], device_id=((o + do) % NO, z, (r + dr) % NR), device_id_type=MESH)

    def relay(zz):
        @pl.when(relays)
        def _():
            for v in ORDER[zz]:
                arrival = pltpu.make_async_remote_copy(
                    src_ref=masked.at[0], dst_ref=ints.at[v, r, half], send_sem=mine_send.at[0],
                    recv_sem=mine_recv.at[v], device_id=((o + 1) % NO, z, r), device_id_type=MESH)
                if v == zz:
                    @pl.when(o != z)
                    def _():
                        arrival.wait_recv()
                else:
                    arrival.wait_recv()
                for k in range(len(PEERS)):
                    hand(v, k).start()

    def gathered(v):
        for rr in range(NR):
            for h in range(2):
                @pl.when(jnp.logical_not(relays & (r == rr) & (half == h)))
                def _():
                    pltpu.make_async_remote_copy(
                        src_ref=ints.at[v, rr, h], dst_ref=ints.at[v, rr, h], send_sem=relay_send.at[v, 0],
                        recv_sem=relay_recv.at[v, rr, h], device_id=((o + 1) % NO, z, r),
                        device_id_type=MESH).wait_recv()
                full[v, rr * part:(rr + 1) * part, h * width:(h + 1) * width] = ints[v, rr, h]

    def pass_on(zz, v, c):
        to = zz + 1 if v > zz else zz - 1
        slot = NV if (v < zz and v == to) else v
        where = dict(device_id=(o, to, r), device_id_type=MESH)
        return (
            pltpu.make_async_remote_copy(
                src_ref=psend.at[v, c], dst_ref=precv.at[slot, c], send_sem=p_ssem.at[v, c],
                recv_sem=p_rsem.at[slot, c], **where),
            pltpu.make_async_remote_copy(
                src_ref=ssend.at[v, c], dst_ref=srecv.at[slot, c], send_sem=s_ssem.at[v, c],
                recv_sem=s_rsem.at[slot, c], **where),
        )

    def arrived(slot, c):
        where = dict(device_id=(o, (z + 1) % NV, r), device_id_type=MESH)
        pltpu.make_async_remote_copy(
            src_ref=precv.at[slot, c], dst_ref=precv.at[slot, c], send_sem=p_ssem.at[0, c],
            recv_sem=p_rsem.at[slot, c], **where).wait_recv()
        pltpu.make_async_remote_copy(
            src_ref=srecv.at[slot, c], dst_ref=srecv.at[slot, c], send_sem=s_ssem.at[0, c],
            recv_sem=s_rsem.at[slot, c], **where).wait_recv()
        return precv[slot, c].astype(jnp.int32).astype(jnp.float32) * srecv[slot, c, 0:1, :]

    def line(zz):
        relay(zz)
        seen = set()
        for v, c in schedule(zz):
            if v not in seen:
                gathered(v)
                seen.add(v)
            at = slice(c * chunk, (c + 1) * chunk)
            total = jnp.dot(t_ref[at, :], full[v], preferred_element_type=jnp.float32)
            if v >= zz and zz > 0:
                total += arrived(v, c)
            if v < zz and zz < NV - 1:
                total += arrived(v, c)
            if v == zz and zz < NV - 1:
                total += arrived(NV, c)
            if v == zz:
                out_ref[at, :] = total
            else:
                most = jnp.maximum(jnp.max(jnp.abs(total), axis=0, keepdims=True), 1e-30)
                ssend[v, c] = jnp.broadcast_to(most * (1.0 / 32767.0), (8, total.shape[1]))
                psend[v, c] = jnp.round(total * (32767.0 / most)).astype(jnp.int32).astype(jnp.int16)
                for copy in pass_on(zz, v, c):
                    copy.start()
        for v, c in schedule(zz):
            if v != zz:
                for copy in pass_on(zz, v, c):
                    copy.wait_send()

        @pl.when(relays)
        def _():
            for v in ORDER[zz]:
                for k in range(len(PEERS)):
                    hand(v, k).wait_send()

    for zz in range(NV):
        @pl.when(z == zz)
        def _():
            line(zz)

    for h in range(2):
        @pl.when(jnp.logical_not(stays[h]))
        def _():
            first(h).wait_send()


def on_lines(amplitudes, integrals, cd_irrep, ab_irrep):
    rows, depth = amplitudes.shape
    part, width = integrals.shape
    chunk = rows // CHUNKS
    slots = NV + 1
    dma = pltpu.SemaphoreType.DMA
    return pl.pallas_call(
        kernel,
        out_shape=jax.ShapeDtypeStruct((rows, width), jnp.float32),
        in_specs=[pl.BlockSpec(memory_space=pltpu.VMEM)] * 4,
        out_specs=pl.BlockSpec(memory_space=pltpu.VMEM),
        scratch_shapes=[
            pltpu.VMEM((2, part, width // 2), jnp.bfloat16),
            pltpu.VMEM((NV, NR, 2, part, width // 2), jnp.bfloat16),
            pltpu.VMEM((NV, depth, width), jnp.bfloat16),
            pltpu.VMEM((NV, CHUNKS, chunk, width), jnp.int16),
            pltpu.VMEM((NV, CHUNKS, 8, width), jnp.float32),
            pltpu.VMEM((slots, CHUNKS, chunk, width), jnp.int16),
            pltpu.VMEM((slots, CHUNKS, 8, width), jnp.float32),
            dma((2,)), dma((NV,)), dma((NV, len(PEERS))), dma((NV, NR, 2)),
            dma((NV, CHUNKS)), dma((NV, CHUNKS)), dma((slots, CHUNKS)), dma((slots, CHUNKS)),
        ],
        compiler_params=pltpu.CompilerParams(
            collective_id=0, has_side_effects=True, vmem_limit_bytes=32 * 1024 * 1024),
        cost_estimate=pl.CostEstimate(
            flops=2 * rows * depth * NV * width, bytes_accessed=3 * rows * depth, transcendentals=0),
    )(amplitudes, integrals, cd_irrep.reshape(1, -1), ab_irrep.reshape(1, -1))


def by_gathers(amplitudes, integrals, cd_irrep, ab_irrep):
    allowed = cd_irrep[:, None] == ab_irrep[None, :]
    masked = jnp.where(allowed, integrals, jnp.zeros_like(integrals))
    rows = lax.all_gather(masked, ("occ", "rep"), axis=0, tiled=True)
    columns = lax.all_gather(amplitudes, "virt", axis=1, tiled=True)
    return jnp.dot(columns, rows, preferred_element_type=jnp.float32)


def solution(mesh):
    in_specs = (P(("occ", "rep"), "virt"), P(("occ", "rep"), "virt"), P(("occ", "rep")), P("virt"))
    out_specs = P(("occ", "rep"), "virt")
    lines = (mesh.shape["occ"], mesh.shape["virt"], mesh.shape["rep"]) == (NO, NV, NR)
    return jax.shard_map(on_lines if lines else by_gathers, mesh=mesh, in_specs=in_specs,
                         out_specs=out_specs, check_vma=False)
```

```python
import functools

import jax
import jax.numpy as jnp
from jax import lax
from jax.experimental import pallas as pl
from jax.experimental.pallas import tpu as pltpu
from jax.sharding import PartitionSpec as P

MESH = pl.DeviceIdType.MESH
NV = 4
NO = 4
NR = 2
CHUNKS = 4
ORDER = ((3, 2, 1, 0), (3, 0, 2, 1), (0, 3, 1, 2), (0, 1, 2, 3))
PEERS = [(2, 0), (0, 1), (2, 1)]


def parts_of(zz, v):
    chunks = list(range(CHUNKS))
    late = v == zz or 0 < v < NV - 1
    return chunks[CHUNKS // 2:] + chunks[:CHUNKS // 2] if late else chunks


def schedule(zz):
    steps = []
    if zz in (0, NV - 1):
        for v in ORDER[zz][:-1]:
            steps += [(v, c) for c in parts_of(zz, v)]
    else:
        a, b, near, _ = ORDER[zz]
        timed = []
        for k in range(CHUNKS):
            timed += [(k, 0, a, parts_of(zz, a)[k]), (k + 1.5, 1, b, parts_of(zz, b)[k]),
                      (k + CHUNKS + 0.7, 2, near, parts_of(zz, near)[k])]
        steps = [(v, c) for _, _, v, c in sorted(timed)]
    return steps + [(zz, c) for c in parts_of(zz, zz)]


def kernel(t_ref, i_ref, cd_ref, ab_ref, out_ref, masked, both, ints, full, psend, ssend, precv, srecv, fin,
           mine_send, mine_recv, relay_send, relay_recv, p_ssem, s_ssem, p_rsem, s_rsem, t_sem, f_ssem, f_rsem):
    o, z, r = lax.axis_index("occ"), lax.axis_index("virt"), lax.axis_index("rep")
    core = o % 2
    half = o // 2
    other = 2 * half + 1 - core
    rows, depth = t_ref.shape
    chunk = 2 * rows // CHUNKS
    part = depth // NR

    barrier = pltpu.get_barrier_semaphore()
    friends = 0
    for dz in range(NV):
        for do in range(NO):
            if (dz, do) != (0, 0):
                pl.semaphore_signal(
                    barrier, inc=1, device_id=((o + do) % NO, (z + dz) % NV, r), device_id_type=MESH)
                friends += 1
    for do in (0, 2):
        pl.semaphore_signal(barrier, inc=1, device_id=((o + do) % NO, z, (r + 1) % NR), device_id_type=MESH)
        friends += 1

    cd = cd_ref[...]
    ab = ab_ref[...]
    one_cd = (lax.broadcasted_iota(jnp.int32, (8, cd.shape[1]), 0) == cd).astype(jnp.float32)
    one_ab = (lax.broadcasted_iota(jnp.int32, (8, ab.shape[1]), 0) == ab).astype(jnp.float32)
    same = lax.dot_general(one_cd, one_ab, (((0,), (0,)), ((), ())), preferred_element_type=jnp.float32)
    kept = jnp.where(same > 0.5, i_ref[...].astype(jnp.float32), 0.0).astype(jnp.bfloat16)
    width = kept.shape[1] // 2
    masked[0] = kept[:, :width]
    masked[1] = kept[:, width:]
    both[core] = t_ref[...]

    pl.semaphore_wait(barrier, friends)

    def first(h):
        return pltpu.make_async_remote_copy(
            src_ref=masked.at[h], dst_ref=ints.at[z, r], send_sem=mine_send.at[h], recv_sem=mine_recv.at[z],
            device_id=(3 * h, o, r), device_id_type=MESH)

    stays = [(z == o) & (o == 3 * h) for h in range(2)]
    for h in range(2):
        @pl.when(jnp.logical_not(stays[h]))
        def _():
            first(h).start()

        @pl.when(stays[h])
        def _():
            ints[z, r] = masked[h]

    def share(k):
        return pltpu.make_async_remote_copy(
            src_ref=both.at[k], dst_ref=both.at[k], send_sem=t_sem.at[0], recv_sem=t_sem.at[1],
            device_id=(other, z, r), device_id_type=MESH)

    share(core).start()

    relays = core == half

    def hand(v, k):
        do, dr = PEERS[k]
        return pltpu.make_async_remote_copy(
            src_ref=ints.at[v, r], dst_ref=ints.at[v, r], send_sem=relay_send.at[v, k],
            recv_sem=relay_recv.at[v, r], device_id=((o + do) % NO, z, (r + dr) % NR), device_id_type=MESH)

    def relay(zz, v):
        @pl.when(relays)
        def _():
            arrival = pltpu.make_async_remote_copy(
                src_ref=masked.at[0], dst_ref=ints.at[v, r], send_sem=mine_send.at[0],
                recv_sem=mine_recv.at[v], device_id=(other, z, r), device_id_type=MESH)
            if v == zz:
                @pl.when(o != z)
                def _():
                    arrival.wait_recv()
            else:
                arrival.wait_recv()
            for k in range(len(PEERS)):
                hand(v, k).start()

    def gathered(v):
        for rr in range(NR):
            @pl.when(jnp.logical_not(relays & (r == rr)))
            def _():
                pltpu.make_async_remote_copy(
                    src_ref=ints.at[v, rr], dst_ref=ints.at[v, rr], send_sem=relay_send.at[v, 0],
                    recv_sem=relay_recv.at[v, rr], device_id=(other, z, r), device_id_type=MESH).wait_recv()
            full[v, rr * part:(rr + 1) * part, :] = ints[v, rr]

    def pass_on(zz, v, c):
        to = zz + 1 if v > zz else zz - 1
        slot = NV if (v < zz and v == to) else v
        where = dict(device_id=(o, to, r), device_id_type=MESH)
        return (
            pltpu.make_async_remote_copy(
                src_ref=psend.at[v, c], dst_ref=precv.at[slot, c], send_sem=p_ssem.at[v, c],
                recv_sem=p_rsem.at[slot, c], **where),
            pltpu.make_async_remote_copy(
                src_ref=ssend.at[v, c], dst_ref=srecv.at[slot, c], send_sem=s_ssem.at[v, c],
                recv_sem=s_rsem.at[slot, c], **where),
        )

    def arrived(slot, c):
        where = dict(device_id=(other, z, r), device_id_type=MESH)
        pltpu.make_async_remote_copy(
            src_ref=precv.at[slot, c], dst_ref=precv.at[slot, c], send_sem=p_ssem.at[0, c],
            recv_sem=p_rsem.at[slot, c], **where).wait_recv()
        pltpu.make_async_remote_copy(
            src_ref=srecv.at[slot, c], dst_ref=srecv.at[slot, c], send_sem=s_ssem.at[0, c],
            recv_sem=s_rsem.at[slot, c], **where).wait_recv()
        return precv[slot, c].astype(jnp.int32).astype(jnp.float32) * srecv[slot, c, 0:1, :]

    def finish(hh, j):
        return pltpu.make_async_remote_copy(
            src_ref=fin.at[j], dst_ref=out_ref.at[j * chunk:(j + 1) * chunk, hh * width:(hh + 1) * width],
            send_sem=f_ssem.at[j], recv_sem=f_rsem.at[j], device_id=(other, z, r), device_id_type=MESH)

    per = CHUNKS // 2

    def line(zz):
        order = list(ORDER[zz])
        ahead = 2 if zz in (0, NV - 1) else NV
        for v in order[:ahead]:
            relay(zz, v)
        waiting = order[ahead:]
        seen, shared = set(), False
        for v, c in schedule(zz):
            if v not in seen:
                gathered(v)
                seen.add(v)
            cc, j = (core + c // per) % 2, c % per
            if c >= per and not shared:
                share(1 - core).wait_recv()
                shared = True
            total = jnp.dot(both[cc, j * chunk:(j + 1) * chunk, :], full[v], preferred_element_type=jnp.float32)
            if v >= zz and zz > 0:
                total += arrived(v, c)
            if v < zz and zz < NV - 1:
                total += arrived(v, c)
            if v == zz and zz < NV - 1:
                total += arrived(NV, c)
            if v == zz:
                for hh in range(2):
                    @pl.when(core == hh)
                    def _():
                        if c < per:
                            out_ref[j * chunk:(j + 1) * chunk, hh * width:(hh + 1) * width] = total
                        else:
                            fin[j] = total
                            finish(hh, j).start()
            else:
                most = jnp.maximum(jnp.max(jnp.abs(total), axis=0, keepdims=True), 1e-30)
                ssend[v, c] = jnp.broadcast_to(most * (1.0 / 32767.0), (8, total.shape[1]))
                psend[v, c] = jnp.round(total * (32767.0 / most)).astype(jnp.int32).astype(jnp.int16)
                for copy in pass_on(zz, v, c):
                    copy.start()
            if waiting and c == parts_of(zz, v)[-1]:
                relay(zz, waiting.pop(0))
        for v, c in schedule(zz):
            if v != zz:
                for copy in pass_on(zz, v, c):
                    copy.wait_send()

        @pl.when(relays)
        def _():
            for v in ORDER[zz]:
                for k in range(len(PEERS)):
                    hand(v, k).wait_send()

    for zz in range(NV):
        @pl.when(z == zz)
        def _():
            line(zz)

    for h in range(2):
        @pl.when(jnp.logical_not(stays[h]))
        def _():
            first(h).wait_send()
    share(core).wait_send()
    for hh in range(2):
        @pl.when(core == hh)
        def _():
            for j in range(per):
                finish(hh, j).wait_send()
                finish(1 - hh, j).wait_recv()


def on_lines(amplitudes, integrals, cd_irrep, ab_irrep):
    rows, depth = amplitudes.shape
    part, width = integrals.shape
    chunk, half = 2 * rows // CHUNKS, width // 2
    slots = NV + 1
    dma = pltpu.SemaphoreType.DMA
    return pl.pallas_call(
        kernel,
        out_shape=jax.ShapeDtypeStruct((rows, width), jnp.float32),
        in_specs=[pl.BlockSpec(memory_space=pltpu.VMEM)] * 4,
        out_specs=pl.BlockSpec(memory_space=pltpu.VMEM),
        scratch_shapes=[
            pltpu.VMEM((2, part, half), jnp.bfloat16),
            pltpu.VMEM((2, rows, depth), jnp.bfloat16),
            pltpu.VMEM((NV, NR, part, half), jnp.bfloat16),
            pltpu.VMEM((NV, depth, half), jnp.bfloat16),
            pltpu.VMEM((NV, CHUNKS, chunk, half), jnp.int16),
            pltpu.VMEM((NV, CHUNKS, 8, half), jnp.float32),
            pltpu.VMEM((slots, CHUNKS, chunk, half), jnp.int16),
            pltpu.VMEM((slots, CHUNKS, 8, half), jnp.float32),
            pltpu.VMEM((CHUNKS // 2, chunk, half), jnp.float32),
            dma((2,)), dma((NV,)), dma((NV, len(PEERS))), dma((NV, NR)),
            dma((NV, CHUNKS)), dma((NV, CHUNKS)), dma((slots, CHUNKS)), dma((slots, CHUNKS)),
            dma((2,)), dma((CHUNKS // 2,)), dma((CHUNKS // 2,)),
        ],
        compiler_params=pltpu.CompilerParams(
            collective_id=0, has_side_effects=True, vmem_limit_bytes=32 * 1024 * 1024),
        cost_estimate=pl.CostEstimate(
            flops=2 * rows * depth * NV * width, bytes_accessed=3 * rows * depth, transcendentals=0),
    )(amplitudes, integrals, cd_irrep.reshape(1, -1), ab_irrep.reshape(1, -1))


def by_gathers(amplitudes, integrals, cd_irrep, ab_irrep):
    allowed = cd_irrep[:, None] == ab_irrep[None, :]
    masked = jnp.where(allowed, integrals, jnp.zeros_like(integrals))
    rows = lax.all_gather(masked, ("occ", "rep"), axis=0, tiled=True)
    columns = lax.all_gather(amplitudes, "virt", axis=1, tiled=True)
    return jnp.dot(columns, rows, preferred_element_type=jnp.float32)


def solution(mesh):
    in_specs = (P(("occ", "rep"), "virt"), P(("occ", "rep"), "virt"), P(("occ", "rep")), P("virt"))
    out_specs = P(("occ", "rep"), "virt")
    lines = (mesh.shape["occ"], mesh.shape["virt"], mesh.shape["rep"]) == (NO, NV, NR)
    return jax.shard_map(on_lines if lines else by_gathers, mesh=mesh, in_specs=in_specs,
                         out_specs=out_specs, check_vma=False)
```

```python
import functools

import jax
import jax.numpy as jnp
from jax import lax
from jax.experimental import pallas as pl
from jax.experimental.pallas import tpu as pltpu
from jax.sharding import PartitionSpec as P

MESH = pl.DeviceIdType.MESH
NV = 4
NO = 4
NR = 2
CHUNKS = 4
ORDER = ((2, 3, 1, 0), (2, 3, 0, 1), (1, 0, 3, 2), (1, 0, 2, 3))
PEERS = [(2, 0), (0, 1), (2, 1)]


def parts_of(zz, v):
    chunks = list(range(CHUNKS))
    late = v == zz or 0 < v < NV - 1
    return chunks[CHUNKS // 2:] + chunks[:CHUNKS // 2] if late else chunks


def schedule(zz):
    steps = []
    if zz in (0, NV - 1):
        for v in ORDER[zz][:-1]:
            steps += [(v, c) for c in parts_of(zz, v)]
    else:
        a, b, back, _ = ORDER[zz]
        timed = []
        for k in range(CHUNKS):
            timed += [(k, 0, a, parts_of(zz, a)[k]), (k + CHUNKS + 0.7, 1, b, parts_of(zz, b)[k]),
                      (k + CHUNKS + 2, 2, back, parts_of(zz, back)[k])]
        steps = [(v, c) for _, _, v, c in sorted(timed)]
    return steps + [(zz, c) for c in parts_of(zz, zz)]


def kernel(t_ref, i_ref, cd_ref, ab_ref, out_ref, masked, both, ints, full, psend, ssend, precv, srecv, fin,
           mine_send, mine_recv, relay_send, relay_recv, p_ssem, s_ssem, p_rsem, s_rsem, t_sem, f_ssem, f_rsem):
    o, z, r = lax.axis_index("occ"), lax.axis_index("virt"), lax.axis_index("rep")
    core = o % 2
    half = o // 2
    other = 2 * half + 1 - core
    rows, depth = t_ref.shape
    chunk = 2 * rows // CHUNKS
    part = depth // NR

    barrier = pltpu.get_barrier_semaphore()
    friends = 0
    for dz in range(NV):
        for do in range(NO):
            if (dz, do) != (0, 0):
                pl.semaphore_signal(
                    barrier, inc=1, device_id=((o + do) % NO, (z + dz) % NV, r), device_id_type=MESH)
                friends += 1
    for do in (0, 2):
        pl.semaphore_signal(barrier, inc=1, device_id=((o + do) % NO, z, (r + 1) % NR), device_id_type=MESH)
        friends += 1

    cd = cd_ref[...]
    ab = ab_ref[...]
    one_cd = (lax.broadcasted_iota(jnp.int32, (8, cd.shape[1]), 0) == cd).astype(jnp.float32)
    one_ab = (lax.broadcasted_iota(jnp.int32, (8, ab.shape[1]), 0) == ab).astype(jnp.float32)
    same = lax.dot_general(one_cd, one_ab, (((0,), (0,)), ((), ())), preferred_element_type=jnp.float32)
    kept = jnp.where(same > 0.5, i_ref[...].astype(jnp.float32), 0.0).astype(jnp.bfloat16)
    width = kept.shape[1] // 2
    masked[0] = kept[:, :width]
    masked[1] = kept[:, width:]
    both[core] = t_ref[...]

    pl.semaphore_wait(barrier, friends)

    def first(h):
        return pltpu.make_async_remote_copy(
            src_ref=masked.at[h], dst_ref=ints.at[z, r], send_sem=mine_send.at[h], recv_sem=mine_recv.at[z],
            device_id=(3 * h, o, r), device_id_type=MESH)

    stays = [(z == o) & (o == 3 * h) for h in range(2)]
    for h in range(2):
        @pl.when(jnp.logical_not(stays[h]))
        def _():
            first(h).start()

        @pl.when(stays[h])
        def _():
            ints[z, r] = masked[h]

    def share(k):
        return pltpu.make_async_remote_copy(
            src_ref=both.at[k], dst_ref=both.at[k], send_sem=t_sem.at[0], recv_sem=t_sem.at[1],
            device_id=(other, z, r), device_id_type=MESH)

    share(core).start()

    relays = core == half

    def hand(v, k):
        do, dr = PEERS[k]
        return pltpu.make_async_remote_copy(
            src_ref=ints.at[v, r], dst_ref=ints.at[v, r], send_sem=relay_send.at[v, k],
            recv_sem=relay_recv.at[v, r], device_id=((o + do) % NO, z, (r + dr) % NR), device_id_type=MESH)

    def relay(zz, v):
        @pl.when(relays)
        def _():
            arrival = pltpu.make_async_remote_copy(
                src_ref=masked.at[0], dst_ref=ints.at[v, r], send_sem=mine_send.at[0],
                recv_sem=mine_recv.at[v], device_id=(other, z, r), device_id_type=MESH)
            if v == zz:
                @pl.when(o != z)
                def _():
                    arrival.wait_recv()
            else:
                arrival.wait_recv()
            for k in range(len(PEERS)):
                hand(v, k).start()

    def gathered(v):
        for rr in range(NR):
            @pl.when(jnp.logical_not(relays & (r == rr)))
            def _():
                pltpu.make_async_remote_copy(
                    src_ref=ints.at[v, rr], dst_ref=ints.at[v, rr], send_sem=relay_send.at[v, 0],
                    recv_sem=relay_recv.at[v, rr], device_id=(other, z, r), device_id_type=MESH).wait_recv()
            full[v, rr * part:(rr + 1) * part, :] = ints[v, rr]

    def pass_on(zz, v, c):
        to = zz + 1 if v > zz else zz - 1
        slot = NV if (v < zz and v == to) else v
        where = dict(device_id=(o, to, r), device_id_type=MESH)
        return (
            pltpu.make_async_remote_copy(
                src_ref=psend.at[v, c], dst_ref=precv.at[slot, c], send_sem=p_ssem.at[v, c],
                recv_sem=p_rsem.at[slot, c], **where),
            pltpu.make_async_remote_copy(
                src_ref=ssend.at[v, c], dst_ref=srecv.at[slot, c], send_sem=s_ssem.at[v, c],
                recv_sem=s_rsem.at[slot, c], **where),
        )

    def arrived(slot, c):
        where = dict(device_id=(other, z, r), device_id_type=MESH)
        pltpu.make_async_remote_copy(
            src_ref=precv.at[slot, c], dst_ref=precv.at[slot, c], send_sem=p_ssem.at[0, c],
            recv_sem=p_rsem.at[slot, c], **where).wait_recv()
        pltpu.make_async_remote_copy(
            src_ref=srecv.at[slot, c], dst_ref=srecv.at[slot, c], send_sem=s_ssem.at[0, c],
            recv_sem=s_rsem.at[slot, c], **where).wait_recv()
        return precv[slot, c].astype(jnp.int32).astype(jnp.float32) * srecv[slot, c, 0:1, :]

    def finish(hh, j):
        return pltpu.make_async_remote_copy(
            src_ref=fin.at[j], dst_ref=out_ref.at[j * chunk:(j + 1) * chunk, hh * width:(hh + 1) * width],
            send_sem=f_ssem.at[j], recv_sem=f_rsem.at[j], device_id=(other, z, r), device_id_type=MESH)

    per = CHUNKS // 2

    def line(zz):
        order = list(ORDER[zz])
        ahead = 2 if zz in (0, NV - 1) else NV
        for v in order[:ahead]:
            relay(zz, v)
        waiting = order[ahead:]
        seen, shared = set(), False
        for v, c in schedule(zz):
            if v not in seen:
                gathered(v)
                seen.add(v)
            cc, j = (core + c // per) % 2, c % per
            if c >= per and not shared:
                share(1 - core).wait_recv()
                shared = True
            total = jnp.dot(both[cc, j * chunk:(j + 1) * chunk, :], full[v], preferred_element_type=jnp.float32)
            if v >= zz and zz > 0:
                total += arrived(v, c)
            if v < zz and zz < NV - 1:
                total += arrived(v, c)
            if v == zz and zz < NV - 1:
                total += arrived(NV, c)
            if v == zz:
                for hh in range(2):
                    @pl.when(core == hh)
                    def _():
                        if c < per:
                            out_ref[j * chunk:(j + 1) * chunk, hh * width:(hh + 1) * width] = total
                        else:
                            fin[j] = total
                            finish(hh, j).start()
            else:
                most = jnp.maximum(jnp.max(jnp.abs(total), axis=0, keepdims=True), 1e-30)
                ssend[v, c] = jnp.broadcast_to(most * (1.0 / 32767.0), (8, total.shape[1]))
                psend[v, c] = jnp.round(total * (32767.0 / most)).astype(jnp.int32).astype(jnp.int16)
                for copy in pass_on(zz, v, c):
                    copy.start()
            if waiting and c == parts_of(zz, v)[-1]:
                relay(zz, waiting.pop(0))
        for v, c in schedule(zz):
            if v != zz:
                for copy in pass_on(zz, v, c):
                    copy.wait_send()

        @pl.when(relays)
        def _():
            for v in ORDER[zz]:
                for k in range(len(PEERS)):
                    hand(v, k).wait_send()

    for zz in range(NV):
        @pl.when(z == zz)
        def _():
            line(zz)

    for h in range(2):
        @pl.when(jnp.logical_not(stays[h]))
        def _():
            first(h).wait_send()
    share(core).wait_send()
    for hh in range(2):
        @pl.when(core == hh)
        def _():
            for j in range(per):
                finish(hh, j).wait_send()
                finish(1 - hh, j).wait_recv()


def on_lines(amplitudes, integrals, cd_irrep, ab_irrep):
    rows, depth = amplitudes.shape
    part, width = integrals.shape
    chunk, half = 2 * rows // CHUNKS, width // 2
    slots = NV + 1
    dma = pltpu.SemaphoreType.DMA
    return pl.pallas_call(
        kernel,
        out_shape=jax.ShapeDtypeStruct((rows, width), jnp.float32),
        in_specs=[pl.BlockSpec(memory_space=pltpu.VMEM)] * 4,
        out_specs=pl.BlockSpec(memory_space=pltpu.VMEM),
        scratch_shapes=[
            pltpu.VMEM((2, part, half), jnp.bfloat16),
            pltpu.VMEM((2, rows, depth), jnp.bfloat16),
            pltpu.VMEM((NV, NR, part, half), jnp.bfloat16),
            pltpu.VMEM((NV, depth, half), jnp.bfloat16),
            pltpu.VMEM((NV, CHUNKS, chunk, half), jnp.int16),
            pltpu.VMEM((NV, CHUNKS, 8, half), jnp.float32),
            pltpu.VMEM((slots, CHUNKS, chunk, half), jnp.int16),
            pltpu.VMEM((slots, CHUNKS, 8, half), jnp.float32),
            pltpu.VMEM((CHUNKS // 2, chunk, half), jnp.float32),
            dma((2,)), dma((NV,)), dma((NV, len(PEERS))), dma((NV, NR)),
            dma((NV, CHUNKS)), dma((NV, CHUNKS)), dma((slots, CHUNKS)), dma((slots, CHUNKS)),
            dma((2,)), dma((CHUNKS // 2,)), dma((CHUNKS // 2,)),
        ],
        compiler_params=pltpu.CompilerParams(
            collective_id=0, has_side_effects=True, vmem_limit_bytes=32 * 1024 * 1024),
        cost_estimate=pl.CostEstimate(
            flops=2 * rows * depth * NV * width, bytes_accessed=3 * rows * depth, transcendentals=0),
    )(amplitudes, integrals, cd_irrep.reshape(1, -1), ab_irrep.reshape(1, -1))


def by_gathers(amplitudes, integrals, cd_irrep, ab_irrep):
    allowed = cd_irrep[:, None] == ab_irrep[None, :]
    masked = jnp.where(allowed, integrals, jnp.zeros_like(integrals))
    rows = lax.all_gather(masked, ("occ", "rep"), axis=0, tiled=True)
    columns = lax.all_gather(amplitudes, "virt", axis=1, tiled=True)
    return jnp.dot(columns, rows, preferred_element_type=jnp.float32)


def solution(mesh):
    in_specs = (P(("occ", "rep"), "virt"), P(("occ", "rep"), "virt"), P(("occ", "rep")), P("virt"))
    out_specs = P(("occ", "rep"), "virt")
    lines = (mesh.shape["occ"], mesh.shape["virt"], mesh.shape["rep"]) == (NO, NV, NR)
    return jax.shard_map(on_lines if lines else by_gathers, mesh=mesh, in_specs=in_specs,
                         out_specs=out_specs, check_vma=False)
```
